512 devices in a mesh: replica: 64 (over x, z, y_lo), tensor: 8 (over y_hi, core).
Axes of the slice: x: 4, y: 8 (y_hi: 4, y_lo: 2; y = y_hi * 2 + y_lo), z: 8, core: 2. Of those that a mesh axis runs over, the one named last changes fastest.
Arguments:
- global_start: bfloat16 [256, 8192], P(None, 'tensor'), may hold values from -6 to 6
- local_params: bfloat16 [64, 2, 256, 8192], P('replica', None, None, 'tensor'), may hold values from -16 to 16
- layer_index: int32 [64], P('replica'), may hold values from 0 to 1
- momentum: float32 [256, 8192], P('replica', 'tensor'), may hold values from -6 to 6
- queries: bfloat16 [64, 1024, 4096], P('replica', None, 'tensor'), may hold values from -6 to 6
- keyvals: bfloat16 [64, 2, 1024, 1024], P('replica', None, None, 'tensor'), may hold values from -6 to 6
- segment_ids: int32 [64, 1024], P('replica'), may hold values from 0 to 3, never falling along the last dimension, each value on 1 to 512 neighbouring positions
Outputs:
- new_momentum: float32 [256, 8192], P('replica', 'tensor')
- blended: bfloat16 [64, 256, 8192], P('replica', None, 'tensor')
- attended: bfloat16 [64, 1024, 4096], P('replica', None, 'tensor')
The draws below stay inside these ranges and needn't reach their ends.
All inputs are finite; a program needn't handle non-finite values.
Results may differ from the reference program's by a relative error of at most 0.009.
Values may be sent and summed in bfloat16 or wider, within the bound.
A program may use at most 64 MiB of HBM per device.

```python
import math
import jax
import jax.numpy as jnp
import numpy as np
from jax import lax

D = 8192
HEAD = 128
QH_DEV = 4
LEN = 1024
FRAG = 256
LAYERS = 2
REPLICAS = 64
QHEADS = 32
KVHEADS = 8


def marked_rows(key):
    key = jax.random.fold_in(key, 101)
    place_key, sign_key = jax.random.split(key)
    chosen = jax.random.randint(place_key, (REPLICAS, KVHEADS, 4), 1, LEN)
    positions = jnp.arange(LEN, dtype=jnp.int32)
    marked = jnp.any(positions[None, :, None, None] == chosen[:, None, :, :], axis=-1)
    sign_table = jax.random.randint(sign_key, (REPLICAS, LEN, KVHEADS, HEAD), 0, 2).astype(jnp.float32) * 2.0 - 1.0
    return (marked, sign_table)


def base_noise(noise_key, shape):
    return jax.random.truncated_normal(noise_key, -6.0, 6.0, shape, jnp.float32)


def draw_queries(key, part):
    marked, sign_table = marked_rows(key)
    key = jax.random.fold_in(key, 7)
    noise_key, level_key = jax.random.split(key, 2)
    shape = (REPLICAS, LEN, KVHEADS, QH_DEV, HEAD)
    noise = base_noise(noise_key, shape)
    levels = jax.random.randint(level_key, (REPLICAS, LEN, KVHEADS, QH_DEV, 1), 3, 7).astype(jnp.float32)
    aligned = levels * sign_table[:, :, :, None, :]
    result = jnp.where(marked[:, :, :, None, None], aligned, noise)
    return result.reshape(REPLICAS, LEN, QHEADS * HEAD).astype(jnp.bfloat16)


def draw_keyvals(key, part):
    marked, sign_table = marked_rows(key)
    key = jax.random.fold_in(key, 11)
    noise_key = jax.random.fold_in(key, 0)
    shape = (REPLICAS, 2, LEN, KVHEADS, HEAD)
    noise = base_noise(noise_key, shape)
    before = jnp.concatenate([marked[:, 1:], jnp.zeros((REPLICAS, 1, KVHEADS), dtype=bool)], axis=1)
    next_signs = jnp.concatenate([sign_table[:, 1:], jnp.ones((REPLICAS, 1, KVHEADS, HEAD), jnp.float32)], axis=1)
    key_rows = jnp.where(marked[..., None], 5.0 * sign_table, jnp.where(before[..., None], 4.96875 * next_signs, noise[:, 0]))
    result = jnp.stack([key_rows, noise[:, 1]], axis=1)
    return result.reshape(REPLICAS, 2, LEN, KVHEADS * HEAD).astype(jnp.bfloat16)


def plant(values, rng, low, largest):
    dims = values.shape
    spot = [jax.random.randint(jax.random.fold_in(rng, axis), (), 0, dims[axis]) for axis in range(len(dims))]
    values = values.at[tuple(spot)].set(low)
    longest = dims.index(max(dims))
    spot[longest] = (spot[longest] + 1) % dims[longest]
    return values.at[tuple(spot)].set(largest)


def raised(entries, rng, source, target, shards_of, factor):
    def block_of(dim):
        return (jnp.arange(entries.shape[dim]) // (entries.shape[dim] // shards_of)).reshape((-1,) + (1,) * (entries.ndim - 1 - dim))

    one_side = jax.random.permutation(rng, shards_of)[block_of(target)]
    second = (block_of(target) + shards_of // 2) % shards_of
    return jnp.where((block_of(source) == one_side) | (block_of(source) == second), factor * entries, entries)


def block_scale(key, dims, pieces, low, high):
    def one(axis_at, shards_of):
        heights = jax.random.uniform(jax.random.fold_in(jax.random.fold_in(key, 6), axis_at), (shards_of,), jnp.float32, low / len(pieces), high / len(pieces))
        return jnp.repeat(jnp.exp(heights), dims[axis_at] // shards_of).reshape((-1,) + (1,) * (len(dims) - axis_at - 1))

    level = one(*pieces[0])
    for cut in pieces[1:]:
        level = level * one(*cut)
    return level


def profile(count, total, limit, slope):
    loads = [(1 << 20) // math.isqrt(grade ** slope) + 1 for grade in range(2, count + 1)]
    rest, given = total - limit - (count - 1), [1] * (count - 1)
    while rest > 0:
        movable = [i for i in range(count - 1) if given[i] < limit]
        pool, left = sum([loads[i] for i in movable]), rest
        for i in movable:
            more = min(limit - given[i], max(1, left * loads[i] // pool), rest)
            given[i] = given[i] + more
            rest = rest - more
    return np.array([limit] + given)


def ragged(stream_key, number_of, total, most, lean):
    if number_of == 2:
        one = jax.random.randint(stream_key, (), max(1, total - most), min(most, total - 1) + 1)
        return jnp.stack([one, total - one])
    lengths = jnp.asarray(profile(number_of, total, most, lean), jnp.int32)
    twos = (number_of - 1) // 2
    giver, receiver = lengths[1:1 + 2 * twos:2], lengths[2:2 + 2 * twos:2]
    margin = jnp.minimum(giver - 1, most - receiver)
    shifted = jax.random.randint(jax.random.fold_in(stream_key, 1), (twos,), 0, 1 << 20) % (margin + 1)
    lengths = lengths.at[1:1 + 2 * twos:2].set(giver - shifted).at[2:2 + 2 * twos:2].set(receiver + shifted)
    return lengths[jax.random.permutation(jax.random.fold_in(stream_key, 2), number_of)]


def normal_values(key, dims, deviation, bound, shards=(), kind=jnp.bfloat16):
    drawn = jax.random.normal(key, dims, jnp.float32) * deviation
    if len(shards) > 0:
        drawn = block_scale(key, dims, shards, -0.22, 0.18) * drawn
    return jnp.clip(drawn, min=-bound, max=bound).astype(kind)


def heavy_noise(rng, dims, scale, bound, cuts, heavy, held_as=jnp.bfloat16):
    values = scale * jax.random.normal(rng, dims, jnp.float32)
    if cuts:
        values = values * block_scale(rng, dims, cuts, -0.22, 0.18)
    return jnp.clip(raised(values, jax.random.fold_in(rng, 3), *heavy), -bound, bound).astype(held_as)


def setup_inputs(seed: int = 0) -> dict:
    splits = jax.random.split(jax.random.key(seed), 8)
    return {
        "global_start": normal_values(splits[0], (FRAG, D), 1.0, 6.0, ((1, 8),)),
        "local_params": heavy_noise(splits[1], (REPLICAS, LAYERS, FRAG, D), 1.0, 16.0, ((0, 64), (3, 8)), (0, 2, 64, 4.0)),
        "layer_index": plant(jax.random.randint(splits[2], (REPLICAS,), 0, LAYERS), jax.random.fold_in(splits[2], 1), 0, LAYERS - 1).astype(jnp.int32),
        "momentum": normal_values(splits[3], (FRAG, D), 1.0, 6.0, ((0, 64), (1, 8)), jnp.float32),
        "queries": draw_queries(jax.random.fold_in(splits[7], 71), 0),
        "keyvals": draw_keyvals(jax.random.fold_in(splits[7], 71), 0),
        "segment_ids": jax.vmap(lambda own: jnp.searchsorted(jnp.cumsum(ragged(own, 4, LEN, LEN // 2, 1)), jnp.arange(LEN), side="right"))(jax.random.split(splits[6], REPLICAS)).reshape((REPLICAS, LEN)).astype(jnp.int32),
    }


def attend_group(query, keys, values, segment):
    length = query.shape[0]
    block = min(512, length)
    heads = query.shape[1] // keys.shape[1]
    size = keys.shape[1]
    qblocks = query.reshape(length // block, block, heads, size)
    positions = jnp.arange(length, dtype=jnp.int32)
    starts = jnp.arange(length // block, dtype=jnp.int32) * block

    def one_block(args):
        qblock, first = args
        rows = first + jnp.arange(block, dtype=jnp.int32)
        rowseg = lax.dynamic_slice_in_dim(segment, first, block, 0)
        allowed = (rowseg[:, None] == segment[None, :]) & (positions[None, :] <= rows[:, None])
        scores = jnp.einsum('bhd,kd->hbk', qblock.astype(jnp.float32), keys.astype(jnp.float32)) / jnp.sqrt(jnp.float32(size))
        scores = jnp.where(allowed[None], scores, jnp.float32(-1e+30))
        peak = lax.optimization_barrier(jnp.max(scores, axis=-1, keepdims=True))
        expo = jnp.exp(scores - peak)
        probs = (expo / lax.optimization_barrier(jnp.sum(expo, axis=-1, keepdims=True))).astype(jnp.bfloat16)
        out = jnp.einsum('hbk,kd->bhd', probs.astype(jnp.float32), values.astype(jnp.float32))
        return out.astype(jnp.bfloat16).reshape(block, heads * size)
    return lax.map(one_block, (qblocks, starts)).reshape(length, heads * size)

def pick_layer(args):
    stack, slot = args
    return lax.dynamic_index_in_dim(stack, slot, 0, keepdims=False)

def reference(global_start, local_params, layer_index, momentum, queries, keyvals, segment_ids):
    layer = lax.map(pick_layer, (local_params, layer_index.astype(jnp.int32)))
    delta = global_start.astype(jnp.float32)[None] - layer.astype(jnp.float32)
    average = lax.optimization_barrier(jnp.sum(delta, axis=0)) / REPLICAS
    mean_square = jnp.mean(average * average)
    grad = average * lax.rsqrt(mean_square + 1e-06)
    new_momentum = 0.9 * momentum + grad
    new_global = (global_start.astype(jnp.float32) - 0.7 * (grad + 0.9 * new_momentum)).astype(jnp.bfloat16)
    blended = (0.5 * layer.astype(jnp.float32) + 0.5 * new_global.astype(jnp.float32)[None]).astype(jnp.bfloat16)

    def one_replica(args):
        query, keyval, segment = args
        outs = []
        for group in range(KVHEADS):
            qpart = query[:, group * QH_DEV * HEAD:(group + 1) * QH_DEV * HEAD]
            kpart = keyval[0, :, group * HEAD:(group + 1) * HEAD]
            vpart = keyval[1, :, group * HEAD:(group + 1) * HEAD]
            outs.append(attend_group(qpart, kpart, vpart, segment))
        return jnp.concatenate(outs, axis=1)
    attended = lax.map(one_replica, (queries, keyvals, segment_ids))
    return (new_momentum, blended, attended)
```

```python
import jax
import jax.numpy as jnp
from jax import lax
from jax.experimental import pallas as pl
from jax.experimental.pallas import tpu as pltpu
from jax.sharding import PartitionSpec as P

D = 8192
FRAG = 256
REPLICAS = 64
MESH = pl.DeviceIdType.MESH
ROWS = 16
GROUP = 16
TWINS = 4
TENSOR = 8
BLOCK = 256
HEAD = 128
SPAN = 512
F32 = jnp.float32
BF16 = jnp.bfloat16


def fused(
    start_hbm, params_hbm, slot_ref, moment_hbm, query_hbm, keyval_hbm, segment_hbm,
    newmom_ref, blended_ref, attended_ref,
    start, params, layer, moment, query, keyval, segment, values, bias,
    reduce_buf, twin_buf, average, mom_twin, mom_all, mom_full, piece, sum_one, sum_two,
    local_sem, reduce_s, reduce_r, twin_s, twin_r, gather_s, gather_r,
    momone_s, momone_r, momtwo_s, momtwo_r, sumone_s, sumone_r, sumtwo_s, sumtwo_r,
):
    replica = lax.axis_index("replica")
    tensor = lax.axis_index("tensor")
    xs, twin, low = replica // 16, (replica // 4) % TWINS, replica % 4
    mine = xs * 4 + low

    def member(g):
        return ((g // 4) * 16 + twin * 4 + g % 4, tensor)

    def twin_of(t):
        return (xs * 16 + t * 4 + low, tensor)

    def rows_of(g):
        return pl.ds(pl.multiple_of(g * ROWS, ROWS), ROWS)

    def remote(src, dst, send, recv, device):
        return pltpu.make_async_remote_copy(
            src_ref=src, dst_ref=dst, send_sem=send, recv_sem=recv,
            device_id=device, device_id_type=MESH,
        )

    def reduce_copy(k):
        to = (mine + k) % GROUP
        return remote(layer.at[rows_of(to)], reduce_buf.at[mine], reduce_s.at[k], reduce_r.at[mine], member(to))

    def twin_copy(k):
        return remote(twin_buf.at[twin], twin_buf.at[twin], twin_s.at[k], twin_r.at[twin], twin_of((twin + k) % TWINS))

    def gather_copy(k):
        return remote(average.at[mine], average.at[mine], gather_s.at[k], gather_r.at[mine], member((mine + k) % GROUP))

    def momone_copy(k):
        return remote(moment, mom_twin.at[twin], momone_s.at[k], momone_r.at[twin], twin_of((twin + k) % TWINS))

    def momtwo_copy(k):
        return remote(mom_all.at[mine], mom_all.at[mine], momtwo_s.at[k], momtwo_r.at[mine], member((mine + k) % GROUP))

    def sumone_copy(k):
        return remote(
            sum_one.at[tensor], sum_one.at[tensor], sumone_s.at[k], sumone_r.at[tensor],
            (replica, (tensor + k) % TENSOR),
        )

    def sumtwo_copy(k):
        return remote(sum_two.at[mine], sum_two.at[mine], sumtwo_s.at[k], sumtwo_r.at[mine], member((mine + k) % GROUP))

    def each(count, act):
        def step(k, carry):
            act(k)
            return carry
        lax.fori_loop(1, count, step, 0, unroll=True)

    def arrived(slots, sems, slot):
        pltpu.make_async_copy(slots.at[slot], slots.at[slot], sems.at[slot]).wait()

    loads = [
        pltpu.make_async_copy(params_hbm.at[0], params, local_sem.at[0]),
        pltpu.make_async_copy(start_hbm, start, local_sem.at[1]),
        pltpu.make_async_copy(moment_hbm, moment, local_sem.at[2]),
        pltpu.make_async_copy(keyval_hbm.at[0], keyval, local_sem.at[3]),
        pltpu.make_async_copy(segment_hbm, segment, local_sem.at[4]),
        pltpu.make_async_copy(query_hbm.at[0], query, local_sem.at[5]),
    ]
    for load in loads:
        load.start()

    barrier = pltpu.get_barrier_semaphore()

    def greet(device):
        pl.semaphore_signal(barrier, inc=1, device_id=device, device_id_type=MESH)

    each(GROUP, lambda k: greet(member((mine + k) % GROUP)))
    each(TWINS, lambda k: greet(twin_of((twin + k) % TWINS)))
    each(TENSOR, lambda k: greet((replica, (tensor + k) % TENSOR)))

    loads[0].wait()
    slot = slot_ref[0]
    layer[...] = params[slot]
    loads[2].wait()
    pl.semaphore_wait(barrier, GROUP + TWINS + TENSOR - 3)

    each(GROUP, lambda k: reduce_copy(k).start())
    each(TWINS, lambda k: momone_copy(k).start())

    loads[3].wait()
    loads[4].wait()
    loads[5].wait()
    values[:, :HEAD] = keyval[1]
    values[:, HEAD:] = jnp.ones((values.shape[0], HEAD), BF16)
    scale = 1.4426950408889634 / (HEAD ** 0.5)

    def attend(block):
        first, last = block * BLOCK, (block + 1) * BLOCK
        begin = max(0, first - SPAN)
        width = last - begin
        own = jnp.broadcast_to(segment[:, first:last], (BLOCK, BLOCK)).T
        for at in range(begin, last, BLOCK):
            keep = own == segment[:, at:at + BLOCK]
            if at == first:
                row = lax.broadcasted_iota(jnp.int32, (BLOCK, BLOCK), 0)
                col = lax.broadcasted_iota(jnp.int32, (BLOCK, BLOCK), 1)
                keep = keep & (col <= row)
            bias[:, at - begin:at - begin + BLOCK] = jnp.where(keep, 0.0, -1e30).astype(F32)

        def head(h, carry):
            columns = pl.ds(pl.multiple_of(h * HEAD, HEAD), HEAD)
            scores = lax.dot_general(
                query[first:last, columns], keyval[0, begin:last, :],
                (((1,), (1,)), ((), ())), preferred_element_type=F32,
            )
            scores = scores * scale + bias[:, :width]
            peak = jnp.max(scores, axis=1, keepdims=True)
            expo = jnp.exp2(scores - peak).astype(BF16)
            out = jnp.dot(expo, values[begin:last, :], preferred_element_type=F32)
            attended_ref[0, first:last, columns] = (out[:, :HEAD] / out[:, HEAD:]).astype(BF16)
            return carry

        lax.fori_loop(0, query.shape[1] // HEAD, head, 0)

    attend(3)
    attend(2)

    loads[1].wait()
    base = start[rows_of(mine), :].astype(F32)

    def add(k, total):
        place = (mine - k + GROUP) % GROUP
        arrived(reduce_buf, reduce_r, place)
        return total + (base - reduce_buf[place].astype(F32))

    partial = lax.fori_loop(1, GROUP, add, base - layer[rows_of(mine), :].astype(F32), unroll=True)
    twin_buf[twin] = partial.astype(BF16)
    each(TWINS, lambda k: twin_copy(k).start())

    mom_twin[twin] = moment[...]
    each(TWINS, lambda k: arrived(mom_twin, momone_r, (twin + k) % TWINS))
    for t in range(TWINS):
        piece[4 * t:4 * t + 4, :] = mom_twin[t]
    mom_all[mine] = piece[...].astype(BF16)
    each(GROUP, lambda k: momtwo_copy(k).start())

    attend(1)
    attend(0)

    each(TWINS, lambda k: arrived(twin_buf, twin_r, (twin + k) % TWINS))
    total = twin_buf[0].astype(F32)
    for t in range(1, TWINS):
        total = total + twin_buf[t].astype(F32)
    total = total * (1.0 / REPLICAS)
    average[mine] = total.astype(BF16)
    square = total * total
    parts = square[0:8, 0:128]
    for r in range(0, ROWS, 8):
        for c in range(0, square.shape[1], 128):
            if r or c:
                parts = parts + square[r:r + 8, c:c + 128]
    sum_one[tensor] = parts
    each(TENSOR, lambda k: sumone_copy(k).start())
    each(GROUP, lambda k: gather_copy(k).start())

    each(TENSOR, lambda k: arrived(sum_one, sumone_r, (tensor + k) % TENSOR))
    parts = sum_one[0]
    for t in range(1, TENSOR):
        parts = parts + sum_one[t]
    sum_two[mine] = parts
    each(GROUP, lambda k: sumtwo_copy(k).start())

    each(GROUP, lambda k: arrived(mom_all, momtwo_r, (mine - k + GROUP) % GROUP))
    for g in range(GROUP):
        piece[...] = mom_all[g].astype(F32)
        for t in range(TWINS):
            at = (g // 4) * 64 + t * 16 + (g % 4) * 4
            mom_full[at:at + 4, :] = piece[4 * t:4 * t + 4, :]

    each(GROUP, lambda k: arrived(average, gather_r, (mine - k + GROUP) % GROUP))
    each(GROUP, lambda k: arrived(sum_two, sumtwo_r, (mine - k + GROUP) % GROUP))
    parts = sum_two[0]
    for g in range(1, GROUP):
        parts = parts + sum_two[g]
    square = jnp.sum(jnp.sum(parts, axis=1, keepdims=True), axis=0, keepdims=True)
    factor = lax.rsqrt(square * (1.0 / (FRAG * D)) + 1e-06)

    def update(c, carry):
        rows = rows_of(c)
        grad = average[c].astype(F32) * factor
        moved = 0.9 * mom_full[rows, :] + grad
        fresh = (start[rows, :].astype(F32) - 0.7 * (grad + 0.9 * moved)).astype(BF16)
        blended_ref[0, rows, :] = (0.5 * layer[rows, :].astype(F32) + 0.5 * fresh.astype(F32)).astype(BF16)
        return carry

    lax.fori_loop(0, GROUP, update, 0)

    piece[...] = average[replica // 4].astype(F32)
    own = piece[0:4, :]
    for t in range(1, 4):
        own = jnp.where(low == t, piece[4 * t:4 * t + 4, :], own)
    newmom_ref[...] = 0.9 * moment[...] + own * factor

    each(GROUP, lambda k: reduce_copy(k).wait_send())
    each(TWINS, lambda k: twin_copy(k).wait_send())
    each(GROUP, lambda k: gather_copy(k).wait_send())
    each(TWINS, lambda k: momone_copy(k).wait_send())
    each(GROUP, lambda k: momtwo_copy(k).wait_send())
    each(TENSOR, lambda k: sumone_copy(k).wait_send())
    each(GROUP, lambda k: sumtwo_copy(k).wait_send())


def shards(global_start, local_params, layer_index, momentum, queries, keyvals, segment_ids):
    rows, columns = global_start.shape
    length, width = queries.shape[1:]
    whole = pl.BlockSpec(memory_space=pltpu.VMEM)
    far = pl.BlockSpec(memory_space=pl.ANY)
    dma = pltpu.SemaphoreType.DMA
    return pl.pallas_call(
        fused,
        out_shape=(
            jax.ShapeDtypeStruct(momentum.shape, F32),
            jax.ShapeDtypeStruct((1, rows, columns), BF16),
            jax.ShapeDtypeStruct(queries.shape, BF16),
        ),
        in_specs=[far, far, pl.BlockSpec(memory_space=pltpu.SMEM), far, far, far, far],
        out_specs=(whole, whole, whole),
        scratch_shapes=[
            pltpu.VMEM((rows, columns), BF16),
            pltpu.VMEM(local_params.shape[1:], BF16),
            pltpu.VMEM((rows, columns), BF16),
            pltpu.VMEM(momentum.shape, F32),
            pltpu.VMEM((length, width), BF16),
            pltpu.VMEM(keyvals.shape[1:], BF16),
            pltpu.VMEM((1, length), jnp.int32),
            pltpu.VMEM((length, 2 * HEAD), BF16),
            pltpu.VMEM((BLOCK, BLOCK + SPAN), F32),
            pltpu.VMEM((GROUP, ROWS, columns), BF16),
            pltpu.VMEM((TWINS, ROWS, columns), BF16),
            pltpu.VMEM((GROUP, ROWS, columns), BF16),
            pltpu.VMEM((TWINS, 4, columns), F32),
            pltpu.VMEM((GROUP, ROWS, columns), BF16),
            pltpu.VMEM((rows, columns), F32),
            pltpu.VMEM((ROWS, columns), F32),
            pltpu.VMEM((TENSOR, 8, 128), F32),
            pltpu.VMEM((GROUP, 8, 128), F32),
            dma((6,)),
            dma((GROUP,)), dma((GROUP,)),
            dma((TWINS,)), dma((TWINS,)),
            dma((GROUP,)), dma((GROUP,)),
            dma((TWINS,)), dma((TWINS,)),
            dma((GROUP,)), dma((GROUP,)),
            dma((TENSOR,)), dma((TENSOR,)),
            dma((GROUP,)), dma((GROUP,)),
        ],
        compiler_params=pltpu.CompilerParams(
            collective_id=0, has_side_effects=True, vmem_limit_bytes=48 * 1024 * 1024
        ),
    )(global_start, local_params, layer_index, momentum, queries, keyvals, segment_ids)


def solution(mesh):
    in_specs = (
        P(None, "tensor"),
        P("replica", None, None, "tensor"),
        P("replica"),
        P("replica", "tensor"),
        P("replica", None, "tensor"),
        P("replica", None, None, "tensor"),
        P("replica", None),
    )
    out_specs = (P("replica", "tensor"), P("replica", None, "tensor"), P("replica", None, "tensor"))
    return jax.shard_map(shards, mesh=mesh, in_specs=in_specs, out_specs=out_specs, check_vma=False)
```

```python
import jax
import jax.numpy as jnp
from jax import lax
from jax.experimental import pallas as pl
from jax.experimental.pallas import tpu as pltpu
from jax.sharding import PartitionSpec as P

D = 8192
FRAG = 256
REPLICAS = 64
MESH = pl.DeviceIdType.MESH
ROWS = 16
GROUP = 16
TWINS = 4
PLANE = 16
LINE = 8
COLUMN = 8
SHEET = 8
BLOCK = 256
HEAD = 128
SPAN = 512
F32 = jnp.float32
BF16 = jnp.bfloat16


def fused(
    start_hbm, params_hbm, slot_hbm, moment_hbm, query_hbm, keyval_hbm, segment_hbm,
    newmom_hbm, blended_hbm, attended_hbm,
    newmom, blended, attended, slot_ref, start, params, layer, moment, query, keyval, segment, values, bias,
    reduce_buf, twin_buf, average, mom_all, mom_full, piece, sum_one, sum_two,
    local_sem, reduce_s, reduce_r, twin_s, twin_r, gather_s, gather_r,
    momone_s, momone_r, momtwo_s, momtwo_r, sumone_s, sumone_r, sumtwo_s, sumtwo_r,
):
    replica = lax.axis_index("replica")
    tensor = lax.axis_index("tensor")
    xs, twin, low = replica // 16, (replica // 4) % TWINS, replica % 4
    mine = xs * 4 + low
    plane = (replica // 16) * 4 + ((replica // 2) % 2) * 2 + tensor % 2
    line = (tensor // 2) * 2 + replica % 2
    column = (replica // 2) % COLUMN
    sheet = xs * 2 + replica % 2

    def member(g):
        return ((g // 4) * 16 + twin * 4 + g % 4, tensor)

    def twin_of(t):
        return (xs * 16 + t * 4 + low, tensor)

    def plane_of(p):
        return ((p // 4) * 16 + twin * 4 + ((p // 2) % 2) * 2 + replica % 2, (tensor // 2) * 2 + p % 2)

    def line_of(y):
        return ((replica // 2) * 2 + y % 2, (y // 2) * 2 + tensor % 2)

    def column_of(z):
        return (xs * 16 + z * 2 + replica % 2, tensor)

    def sheet_of(p):
        return ((p // 2) * 16 + column * 2 + p % 2, tensor)

    def rows_of(g):
        return pl.ds(pl.multiple_of(g * ROWS, ROWS), ROWS)

    def remote(src, dst, send, recv, device):
        return pltpu.make_async_remote_copy(
            src_ref=src, dst_ref=dst, send_sem=send, recv_sem=recv,
            device_id=device, device_id_type=MESH,
        )

    def reduce_copy(k):
        to = (mine + k) % GROUP
        return remote(layer.at[rows_of(to)], reduce_buf.at[mine], reduce_s.at[k], reduce_r.at[mine], member(to))

    def twin_copy(k):
        return remote(twin_buf.at[twin], twin_buf.at[twin], twin_s.at[k], twin_r.at[twin], twin_of((twin + k) % TWINS))

    def gather_copy(k):
        return remote(average.at[mine], average.at[mine], gather_s.at[k], gather_r.at[mine], member((mine + k) % GROUP))

    def momone_copy(k):
        return remote(
            mom_all.at[sheet, column], mom_all.at[sheet, column], momone_s.at[k], momone_r.at[column],
            column_of((column + k) % COLUMN),
        )

    def momtwo_copy(k):
        return remote(
            mom_all.at[sheet], mom_all.at[sheet], momtwo_s.at[k], momtwo_r.at[sheet], sheet_of((sheet + k) % SHEET)
        )

    def sumone_copy(k):
        return remote(
            sum_one.at[plane], sum_one.at[plane], sumone_s.at[k], sumone_r.at[plane], plane_of((plane + k) % PLANE)
        )

    def sumtwo_copy(k):
        return remote(
            sum_two.at[line], sum_two.at[line], sumtwo_s.at[k], sumtwo_r.at[line], line_of((line + k) % LINE)
        )

    def each(count, act):
        def step(k, carry):
            act(k)
            return carry
        lax.fori_loop(1, count, step, 0, unroll=True)

    def arrived(slots, sems, slot):
        pltpu.make_async_copy(slots.at[slot], slots.at[slot], sems.at[slot]).wait()

    loads = [
        pltpu.make_async_copy(params_hbm.at[0], params, local_sem.at[0]),
        pltpu.make_async_copy(moment_hbm, moment, local_sem.at[1]),
        pltpu.make_async_copy(start_hbm, start, local_sem.at[2]),
        pltpu.make_async_copy(segment_hbm, segment, local_sem.at[3]),
        pltpu.make_async_copy(keyval_hbm.at[0], keyval, local_sem.at[4]),
        pltpu.make_async_copy(query_hbm.at[0], query, local_sem.at[5]),
    ]
    loads[0].start()
    index = pltpu.make_async_copy(slot_hbm, slot_ref, local_sem.at[10])
    index.start()

    barrier = pltpu.get_barrier_semaphore()

    def greet(device):
        pl.semaphore_signal(barrier, inc=1, device_id=device, device_id_type=MESH)

    each(GROUP, lambda k: greet(member((mine + k) % GROUP)))
    each(COLUMN // 2, lambda k: greet(column_of((column + 2 * k) % COLUMN)))
    each(COLUMN // 2, lambda k: greet(column_of((column + 2 * k) % COLUMN // 2 * 2 + 1 - column % 2)))
    for p in range(0, PLANE, 2):
        greet(plane_of(p + 1 - tensor % 2))
    each(LINE // 2, lambda k: greet(line_of((line + 2 * k) % LINE)))
    each(LINE // 2, lambda k: greet(line_of((line + 2 * k) % LINE // 2 * 2 + 1 - line % 2)))
    for load in loads[1:]:
        load.start()

    loads[0].wait()
    index.wait()
    slot = slot_ref[0]
    layer[...] = params[slot]
    loads[1].wait()
    fold = moment.shape[1] // 4
    for j in range(4):
        piece[4 * j:4 * j + 4, :fold] = moment[:, j * fold:(j + 1) * fold]
    mom_all[sheet, column] = piece[:, :fold].astype(BF16)
    pl.semaphore_wait(barrier, GROUP + COLUMN + PLANE // 2 + LINE - 5)

    each(COLUMN, lambda k: momone_copy(k).start())

    each(GROUP, lambda k: reduce_copy(k).start())
    for load in loads[3:]:
        load.wait()
    values[:, :HEAD] = keyval[1]
    values[:, HEAD:] = jnp.ones((values.shape[0], HEAD), BF16)
    scale = 1.4426950408889634 / (HEAD ** 0.5)

    def attend(block):
        first, last = block * BLOCK, (block + 1) * BLOCK
        begin = max(0, first - SPAN)
        width = last - begin
        own = jnp.broadcast_to(segment[:, first:last], (BLOCK, BLOCK)).T
        for at in range(begin, last, BLOCK):
            keep = own == segment[:, at:at + BLOCK]
            if at == first:
                row = lax.broadcasted_iota(jnp.int32, (BLOCK, BLOCK), 0)
                col = lax.broadcasted_iota(jnp.int32, (BLOCK, BLOCK), 1)
                keep = keep & (col <= row)
            bias[:, at - begin:at - begin + BLOCK] = jnp.where(keep, 0.0, -1e30).astype(F32)

        def head(h, carry):
            columns = pl.ds(pl.multiple_of(h * HEAD, HEAD), HEAD)
            scores = lax.dot_general(
                query[first:last, columns], keyval[0, begin:last, :],
                (((1,), (1,)), ((), ())), preferred_element_type=F32,
            )
            scores = scores * scale + bias[:, :width]
            peak = jnp.max(scores, axis=1, keepdims=True)
            expo = jnp.exp2(scores - peak).astype(BF16)
            out = jnp.dot(expo, values[begin:last, :], preferred_element_type=F32)
            attended[first:last, columns] = (out[:, :HEAD] / out[:, HEAD:]).astype(BF16)
            return carry

        lax.fori_loop(0, query.shape[1] // HEAD, head, 0)

    attend(3)
    attend(2)

    loads[2].wait()
    base = start[rows_of(mine), :].astype(F32)

    def add(k, total):
        place = (mine - k + GROUP) % GROUP
        arrived(reduce_buf, reduce_r, place)
        return total + (base - reduce_buf[place].astype(F32))

    partial = lax.fori_loop(1, GROUP, add, base - layer[rows_of(mine), :].astype(F32), unroll=True)
    twin_buf[twin] = partial.astype(BF16)
    each(TWINS, lambda k: twin_copy(k).start())

    each(COLUMN, lambda k: arrived(mom_all.at[sheet], momone_r, (column + k) % COLUMN))
    each(SHEET, lambda k: momtwo_copy(k).start())

    attend(1)
    attend(0)
    attended_out = pltpu.make_async_copy(attended, attended_hbm.at[0], local_sem.at[6])
    attended_out.start()

    each(TWINS, lambda k: arrived(twin_buf, twin_r, (twin + k) % TWINS))
    total = twin_buf[0].astype(F32)
    for t in range(1, TWINS):
        total = total + twin_buf[t].astype(F32)
    total = total * (1.0 / REPLICAS)
    average[mine] = total.astype(BF16)
    square = total * total
    parts = square[0:8, 0:128]
    for r in range(0, ROWS, 8):
        for c in range(0, square.shape[1], 128):
            if r or c:
                parts = parts + square[r:r + 8, c:c + 128]
    sum_one[plane] = parts
    each(PLANE, lambda k: sumone_copy(k).start())
    each(GROUP, lambda k: gather_copy(k).start())

    each(PLANE, lambda k: arrived(sum_one, sumone_r, (plane - k + PLANE) % PLANE))
    parts = sum_one[0]
    for p in range(1, PLANE):
        parts = parts + sum_one[p]
    sum_two[line] = parts
    each(LINE, lambda k: sumtwo_copy(k).start())

    each(SHEET, lambda k: arrived(mom_all, momtwo_r, (sheet - k + SHEET) % SHEET))
    for p in range(SHEET):
        for z in range(COLUMN):
            piece[:, :fold] = mom_all[p, z].astype(F32)
            at = ((p // 2) * 16 + z * 2 + p % 2) * 4
            for j in range(4):
                mom_full[at:at + 4, j * fold:(j + 1) * fold] = piece[4 * j:4 * j + 4, :fold]

    each(GROUP, lambda k: arrived(average, gather_r, (mine - k + GROUP) % GROUP))
    each(LINE, lambda k: arrived(sum_two, sumtwo_r, (line - k + LINE) % LINE))
    parts = sum_two[0]
    for y in range(1, LINE):
        parts = parts + sum_two[y]
    square = jnp.sum(jnp.sum(parts, axis=1, keepdims=True), axis=0, keepdims=True)
    factor = lax.rsqrt(square * (1.0 / (FRAG * D)) + 1e-06)

    def update(c, carry):
        rows = rows_of(c)
        grad = average[c].astype(F32) * factor
        moved = 0.9 * mom_full[rows, :] + grad
        fresh = (start[rows, :].astype(F32) - 0.7 * (grad + 0.9 * moved)).astype(BF16)
        blended[rows, :] = (0.5 * layer[rows, :].astype(F32) + 0.5 * fresh.astype(F32)).astype(BF16)
        return carry

    outs = []
    for part in range(2):
        lax.fori_loop(part * GROUP // 2, (part + 1) * GROUP // 2, update, 0, unroll=True)
        span = pl.ds(part * ROWS * GROUP // 2, ROWS * GROUP // 2)
        outs.append(pltpu.make_async_copy(blended.at[span], blended_hbm.at[0, span], local_sem.at[7 + part]))
        outs[-1].start()

    piece[...] = average[replica // 4].astype(F32)
    own = piece[0:4, :]
    for t in range(1, 4):
        own = jnp.where(low == t, piece[4 * t:4 * t + 4, :], own)
    newmom[...] = 0.9 * moment[...] + own * factor
    outs.append(pltpu.make_async_copy(newmom, newmom_hbm, local_sem.at[9]))
    outs[-1].start()

    each(GROUP, lambda k: reduce_copy(k).wait_send())
    each(TWINS, lambda k: twin_copy(k).wait_send())
    each(GROUP, lambda k: gather_copy(k).wait_send())
    each(COLUMN, lambda k: momone_copy(k).wait_send())
    each(SHEET, lambda k: momtwo_copy(k).wait_send())
    each(PLANE, lambda k: sumone_copy(k).wait_send())
    each(LINE, lambda k: sumtwo_copy(k).wait_send())
    attended_out.wait()
    for out in outs:
        out.wait()


def settle(newmom_in, blended_in, attended_in, newmom_out, blended_out, attended_out, newmom, blended, attended, sem):
    pieces = [(newmom_in, newmom, newmom_out)]
    for source, stage, target in ((attended_in, attended, attended_out), (blended_in, blended, blended_out)):
        for at in range(0, source.shape[1], 256):
            span = pl.ds(at, 256)
            pieces.append((source.at[0, span], stage.at[span], target.at[0, span]))
    into = [pltpu.make_async_copy(p[0], p[1], sem.at[0, i]) for i, p in enumerate(pieces)]
    out = [pltpu.make_async_copy(p[1], p[2], sem.at[1, i]) for i, p in enumerate(pieces)]
    for copy in into:
        copy.start()
    for i in range(len(pieces)):
        into[i].wait()
        out[i].start()
    for copy in out:
        copy.wait()


def shards(global_start, local_params, layer_index, momentum, queries, keyvals, segment_ids):
    rows, columns = global_start.shape
    length, width = queries.shape[1:]
    far = pl.BlockSpec(memory_space=pl.ANY)
    dma = pltpu.SemaphoreType.DMA
    out_shape = (
        jax.ShapeDtypeStruct(momentum.shape, F32),
        jax.ShapeDtypeStruct((1, rows, columns), BF16),
        jax.ShapeDtypeStruct(queries.shape, BF16),
    )
    results = pl.pallas_call(
        fused,
        out_shape=out_shape,
        in_specs=[far, far, far, far, far, far, far],
        out_specs=(far, far, far),
        scratch_shapes=[
            pltpu.VMEM(momentum.shape, F32),
            pltpu.VMEM((rows, columns), BF16),
            pltpu.VMEM((length, width), BF16),
            pltpu.SMEM((1,), jnp.int32),
            pltpu.VMEM((rows, columns), BF16),
            pltpu.VMEM(local_params.shape[1:], BF16),
            pltpu.VMEM((rows, columns), BF16),
            pltpu.VMEM(momentum.shape, F32),
            pltpu.VMEM((length, width), BF16),
            pltpu.VMEM(keyvals.shape[1:], BF16),
            pltpu.VMEM((1, length), jnp.int32),
            pltpu.VMEM((length, 2 * HEAD), BF16),
            pltpu.VMEM((BLOCK, BLOCK + SPAN), F32),
            pltpu.VMEM((GROUP, ROWS, columns), BF16),
            pltpu.VMEM((TWINS, ROWS, columns), BF16),
            pltpu.VMEM((GROUP, ROWS, columns), BF16),
            pltpu.VMEM((SHEET, COLUMN, ROWS, columns // 4), BF16),
            pltpu.VMEM((rows, columns), F32),
            pltpu.VMEM((ROWS, columns), F32),
            pltpu.VMEM((PLANE, 8, 128), F32),
            pltpu.VMEM((LINE, 8, 128), F32),
            dma((11,)),
            dma((GROUP,)), dma((GROUP,)),
            dma((TWINS,)), dma((TWINS,)),
            dma((GROUP,)), dma((GROUP,)),
            dma((COLUMN,)), dma((COLUMN,)),
            dma((SHEET,)), dma((SHEET,)),
            dma((PLANE,)), dma((PLANE,)),
            dma((LINE,)), dma((LINE,)),
        ],
        compiler_params=pltpu.CompilerParams(
            collective_id=0, has_side_effects=True, vmem_limit_bytes=56 * 1024 * 1024
        ),
    )(global_start, local_params, layer_index, momentum, queries, keyvals, segment_ids)
    return pl.pallas_call(
        settle,
        out_shape=out_shape,
        in_specs=[far] * 3,
        out_specs=(far,) * 3,
        scratch_shapes=[
            pltpu.VMEM(momentum.shape, F32),
            pltpu.VMEM((rows, columns), BF16),
            pltpu.VMEM((length, width), BF16),
            dma((2, 6)),
        ],
        compiler_params=pltpu.CompilerParams(vmem_limit_bytes=60 * 1024 * 1024),
    )(*results)


def solution(mesh):
    in_specs = (
        P(None, "tensor"),
        P("replica", None, None, "tensor"),
        P("replica"),
        P("replica", "tensor"),
        P("replica", None, "tensor"),
        P("replica", None, None, "tensor"),
        P("replica", None),
    )
    out_specs = (P("replica", "tensor"), P("replica", None, "tensor"), P("replica", None, "tensor"))
    return jax.shard_map(shards, mesh=mesh, in_specs=in_specs, out_specs=out_specs, check_vma=False)
```

```python
import jax
import jax.numpy as jnp
from jax import lax
from jax.experimental import pallas as pl
from jax.experimental.pallas import tpu as pltpu
from jax.sharding import PartitionSpec as P

D = 8192
FRAG = 256
REPLICAS = 64
MESH = pl.DeviceIdType.MESH
ROWS = 16
GROUP = 16
TWINS = 4
PLANE = 16
LINE = 8
COLUMN = 8
SHEET = 8
BLOCK = 256
HEAD = 128
SPAN = 512
FAR16 = (11, 10, 9, 15, 7, 8, 14, 13, 6, 5, 3, 12, 4, 2, 1)
FAR8 = (4, 3, 5, 2, 6, 1, 7)
FAR4 = (2, 1, 3)
SHEETS = (5, 4, 7, 3, 6, 2, 1)
F32 = jnp.float32
BF16 = jnp.bfloat16


def fused(
    start_hbm, params_hbm, slot_hbm, moment_hbm, query_hbm, keyval_hbm, segment_hbm,
    newmom_hbm, blended_hbm, attended_hbm,
    newmom, blended, attended, slot_ref, start, params, layer, moment, query, keyval, segment, values, bias,
    reduce_buf, twin_buf, average, mom_all, base_full, piece, sum_one, sum_two,
    local_sem, reduce_s, reduce_r, twin_s, twin_r, gather_s, gather_r,
    momone_s, momone_r, momtwo_s, momtwo_r, sumone_s, sumone_r, sumtwo_s, sumtwo_r,
):
    replica = lax.axis_index("replica")
    tensor = lax.axis_index("tensor")
    xs, twin, low = replica // 16, (replica // 4) % TWINS, replica % 4
    mine = xs * 4 + low
    plane = (replica // 16) * 4 + ((replica // 2) % 2) * 2 + tensor % 2
    line = (tensor // 2) * 2 + replica % 2
    column = (replica // 2) % COLUMN
    sheet = xs * 2 + replica % 2

    def member(g):
        return ((g // 4) * 16 + twin * 4 + g % 4, tensor)

    def twin_of(t):
        return (xs * 16 + t * 4 + low, tensor)

    def plane_of(p):
        return ((p // 4) * 16 + twin * 4 + ((p // 2) % 2) * 2 + replica % 2, (tensor // 2) * 2 + p % 2)

    def line_of(y):
        return ((replica // 2) * 2 + y % 2, (y // 2) * 2 + tensor % 2)

    def column_of(z):
        return (xs * 16 + z * 2 + replica % 2, tensor)

    def sheet_of(p):
        return ((p // 2) * 16 + column * 2 + p % 2, tensor)

    def rows_of(g):
        return pl.ds(pl.multiple_of(g * ROWS, ROWS), ROWS)

    def remote(src, dst, send, recv, device):
        return pltpu.make_async_remote_copy(
            src_ref=src, dst_ref=dst, send_sem=send, recv_sem=recv,
            device_id=device, device_id_type=MESH,
        )

    def reduce_copy(k):
        to = off16(mine, k)
        return remote(layer.at[rows_of(to)], reduce_buf.at[mine], reduce_s.at[k], reduce_r.at[mine], member(to))

    def twin_copy(k):
        return remote(twin_buf.at[twin], twin_buf.at[twin], twin_s.at[k], twin_r.at[twin], twin_of((twin + k) % TWINS))

    def gather_copy(k):
        return remote(average.at[mine], average.at[mine], gather_s.at[k], gather_r.at[mine], member(off16(mine, k)))

    def momone_copy(k):
        return remote(
            mom_all.at[sheet, column], mom_all.at[sheet, column], momone_s.at[k], momone_r.at[column],
            column_of((column + k) % COLUMN),
        )

    def momtwo_copy(k):
        return remote(
            mom_all.at[sheet], mom_all.at[sheet], momtwo_s.at[k], momtwo_r.at[sheet], sheet_of(off_sheet(sheet, k))
        )

    def sumone_copy(k):
        return remote(
            sum_one.at[line], sum_one.at[line], sumone_s.at[k], sumone_r.at[line], line_of((line + k) % LINE)
        )

    def sumtwo_copy(k):
        return remote(
            sum_two.at[plane], sum_two.at[plane], sumtwo_s.at[k], sumtwo_r.at[plane], plane_of(off16(plane, k))
        )

    def each(order, act):
        for k in order:
            act(k)

    def off16(place, k):
        return (place // 4 + k // 4) % 4 * 4 + (place // 2 + k // 2) % 2 * 2 + (place + k) % 2

    def back16(place, k):
        return (place // 4 + 4 - k // 4) % 4 * 4 + (place // 2 + k // 2) % 2 * 2 + (place + k) % 2

    def off_sheet(place, k):
        return (place // 2 + k // 2) % 4 * 2 + (place + k) % 2

    def back_sheet(place, k):
        return (place // 2 + 4 - k // 2) % 4 * 2 + (place + k) % 2

    def arrived(slots, sems, slot):
        pltpu.make_async_copy(slots.at[slot], slots.at[slot], sems.at[slot]).wait()

    loads = [
        pltpu.make_async_copy(params_hbm.at[0], params, local_sem.at[0]),
        pltpu.make_async_copy(moment_hbm, moment, local_sem.at[1]),
        pltpu.make_async_copy(start_hbm, start, local_sem.at[2]),
        pltpu.make_async_copy(segment_hbm, segment, local_sem.at[3]),
        pltpu.make_async_copy(keyval_hbm.at[0], keyval, local_sem.at[4]),
        pltpu.make_async_copy(query_hbm.at[0], query, local_sem.at[5]),
    ]
    barrier = pltpu.get_barrier_semaphore()

    def greet(device):
        pl.semaphore_signal(barrier, inc=1, device_id=device, device_id_type=MESH)

    each(FAR16, lambda k: greet(member(off16(mine, k))))
    loads[0].start()
    index = pltpu.make_async_copy(slot_hbm, slot_ref, local_sem.at[10])
    index.start()
    each(FAR4, lambda k: greet(column_of((column + 2 * k) % COLUMN)))
    each(FAR4, lambda k: greet(column_of((column + 2 * k) % COLUMN // 2 * 2 + 1 - column % 2)))
    for p in range(0, PLANE, 2):
        greet(plane_of(p + 1 - tensor % 2))
    each(FAR4, lambda k: greet(line_of((line + 2 * k) % LINE)))
    each(FAR4, lambda k: greet(line_of((line + 2 * k) % LINE // 2 * 2 + 1 - line % 2)))
    for load in loads[1:]:
        load.start()

    loads[0].wait()
    index.wait()
    slot = slot_ref[0]
    layer[...] = params[slot]
    loads[1].wait()
    fold = moment.shape[1] // 4
    for j in range(4):
        piece[4 * j:4 * j + 4, :fold] = moment[:, j * fold:(j + 1) * fold]
    mom_all[sheet, column] = piece[:, :fold].astype(BF16)
    pl.semaphore_wait(barrier, GROUP + COLUMN + PLANE // 2 + LINE - 5)

    each(FAR8, lambda k: momone_copy(k).start())

    each(FAR16, lambda k: reduce_copy(k).start())
    for load in loads[3:]:
        load.wait()
    values[:, :HEAD] = keyval[1]
    values[:, HEAD:] = jnp.ones((values.shape[0], HEAD), BF16)
    scale = 1.4426950408889634 / (HEAD ** 0.5)

    def attend(block):
        first, last = block * BLOCK, (block + 1) * BLOCK
        begin = max(0, first - SPAN)
        width = last - begin
        own = jnp.broadcast_to(segment[:, first:last], (BLOCK, BLOCK)).T
        for at in range(begin, last, BLOCK):
            keep = own == segment[:, at:at + BLOCK]
            if at == first:
                row = lax.broadcasted_iota(jnp.int32, (BLOCK, BLOCK), 0)
                col = lax.broadcasted_iota(jnp.int32, (BLOCK, BLOCK), 1)
                keep = keep & (col <= row)
            bias[:, at - begin:at - begin + BLOCK] = jnp.where(keep, 0.0, -1e30).astype(F32)

        def head(h, carry):
            columns = pl.ds(pl.multiple_of(h * HEAD, HEAD), HEAD)
            scores = lax.dot_general(
                query[first:last, columns], keyval[0, begin:last, :],
                (((1,), (1,)), ((), ())), preferred_element_type=F32,
            )
            scores = scores * scale + bias[:, :width]
            peak = jnp.max(scores, axis=1, keepdims=True)
            expo = jnp.exp2(scores - peak).astype(BF16)
            out = jnp.dot(expo, values[begin:last, :], preferred_element_type=F32)
            attended[first:last, columns] = (out[:, :HEAD] / out[:, HEAD:]).astype(BF16)
            return carry

        lax.fori_loop(0, query.shape[1] // HEAD, head, 0)

    attend(3)
    attend(2)

    loads[2].wait()
    base = start[rows_of(mine), :].astype(F32)

    partial = base - layer[rows_of(mine), :].astype(F32)
    for k in FAR16:
        place = back16(mine, k)
        arrived(reduce_buf, reduce_r, place)
        partial = partial + (base - reduce_buf[place].astype(F32))
    twin_buf[twin] = partial.astype(BF16)
    each(FAR4, lambda k: twin_copy(k).start())

    each(FAR8, lambda k: arrived(mom_all.at[sheet], momone_r, (column - k + COLUMN) % COLUMN))
    each(SHEETS, lambda k: momtwo_copy(k).start())

    attend(1)
    attend(0)
    attended_out = pltpu.make_async_copy(attended, attended_hbm.at[0], local_sem.at[6])
    attended_out.start()

    each(FAR4, lambda k: arrived(twin_buf, twin_r, (twin + TWINS - k) % TWINS))
    total = twin_buf[0].astype(F32)
    for t in range(1, TWINS):
        total = total + twin_buf[t].astype(F32)
    total = total * (1.0 / REPLICAS)
    average[mine] = total.astype(BF16)
    square = total * total
    parts = square[0:8, 0:128]
    for r in range(0, ROWS, 8):
        for c in range(0, square.shape[1], 128):
            if r or c:
                parts = parts + square[r:r + 8, c:c + 128]
    sum_one[line] = jnp.sum(parts, axis=0, keepdims=True)
    each(FAR8, lambda k: sumone_copy(k).start())
    each(FAR16, lambda k: gather_copy(k).start())

    each(FAR8, lambda k: arrived(sum_one, sumone_r, (line - k + LINE) % LINE))
    parts = sum_one[0]
    for y in range(1, LINE):
        parts = parts + sum_one[y]
    sum_two[plane] = parts
    each(FAR16, lambda k: sumtwo_copy(k).start())

    each(SHEETS, lambda k: arrived(mom_all, momtwo_r, back_sheet(sheet, k)))
    for p in range(SHEET):
        for z in range(COLUMN):
            piece[:, :fold] = mom_all[p, z].astype(F32)
            at = ((p // 2) * 16 + z * 2 + p % 2) * 4
            for j in range(4):
                base_full[at:at + 4, j * fold:(j + 1) * fold] = piece[4 * j:4 * j + 4, :fold]

    def ahead(c, carry):
        rows = rows_of(c)
        base_full[rows, :] = start[rows, :].astype(F32) - (0.7 * 0.9 * 0.9) * base_full[rows, :]
        return carry

    lax.fori_loop(0, GROUP, ahead, 0)

    each(FAR16, lambda k: reduce_copy(k).wait_send())
    each(FAR4, lambda k: twin_copy(k).wait_send())
    each(FAR16, lambda k: gather_copy(k).wait_send())
    each(FAR8, lambda k: momone_copy(k).wait_send())
    each(SHEETS, lambda k: momtwo_copy(k).wait_send())
    each(FAR8, lambda k: sumone_copy(k).wait_send())
    each(FAR16, lambda k: arrived(average, gather_r, back16(mine, k)))
    each(FAR16, lambda k: arrived(sum_two, sumtwo_r, back16(plane, k)))
    parts = sum_two[0]
    for p in range(1, PLANE):
        parts = parts + sum_two[p]
    square = jnp.sum(parts, axis=1, keepdims=True)
    factor = lax.rsqrt(square * (1.0 / (FRAG * D)) + 1e-06)
    step = factor * (0.7 * 1.9)

    def update(c, carry):
        rows = rows_of(c)
        fresh = (base_full[rows, :] - average[c].astype(F32) * step).astype(BF16)
        blended[rows, :] = (0.5 * (layer[rows, :].astype(F32) + fresh.astype(F32))).astype(BF16)
        return carry

    outs = []
    for part in range(2):
        lax.fori_loop(part * GROUP // 2, (part + 1) * GROUP // 2, update, 0, unroll=True)
        span = pl.ds(part * ROWS * GROUP // 2, ROWS * GROUP // 2)
        outs.append(pltpu.make_async_copy(blended.at[span], blended_hbm.at[0, span], local_sem.at[7 + part]))
        outs[-1].start()

    piece[...] = average[replica // 4].astype(F32)
    own = piece[0:4, :]
    for t in range(1, 4):
        own = jnp.where(low == t, piece[4 * t:4 * t + 4, :], own)
    newmom[...] = 0.9 * moment[...] + own * factor
    outs.append(pltpu.make_async_copy(newmom, newmom_hbm, local_sem.at[9]))
    outs[-1].start()

    each(FAR16, lambda k: sumtwo_copy(k).wait_send())
    attended_out.wait()
    for out in outs:
        out.wait()


def settle(newmom_in, blended_in, attended_in, newmom_out, blended_out, attended_out, newmom, blended, attended, sem):
    pieces = [(newmom_in, newmom, newmom_out)]
    for source, stage, target in ((attended_in, attended, attended_out), (blended_in, blended, blended_out)):
        for at in range(0, source.shape[1], 256):
            span = pl.ds(at, 256)
            pieces.append((source.at[0, span], stage.at[span], target.at[0, span]))
    into = [pltpu.make_async_copy(p[0], p[1], sem.at[0, i]) for i, p in enumerate(pieces)]
    out = [pltpu.make_async_copy(p[1], p[2], sem.at[1, i]) for i, p in enumerate(pieces)]
    for copy in into:
        copy.start()
    for i in range(len(pieces)):
        into[i].wait()
        out[i].start()
    for copy in out:
        copy.wait()


def shards(global_start, local_params, layer_index, momentum, queries, keyvals, segment_ids):
    rows, columns = global_start.shape
    length, width = queries.shape[1:]
    far = pl.BlockSpec(memory_space=pl.ANY)
    dma = pltpu.SemaphoreType.DMA
    out_shape = (
        jax.ShapeDtypeStruct(momentum.shape, F32),
        jax.ShapeDtypeStruct((1, rows, columns), BF16),
        jax.ShapeDtypeStruct(queries.shape, BF16),
    )
    results = pl.pallas_call(
        fused,
        out_shape=out_shape,
        in_specs=[far, far, far, far, far, far, far],
        out_specs=(far, far, far),
        scratch_shapes=[
            pltpu.VMEM(momentum.shape, F32),
            pltpu.VMEM((rows, columns), BF16),
            pltpu.VMEM((length, width), BF16),
            pltpu.SMEM((1,), jnp.int32),
            pltpu.VMEM((rows, columns), BF16),
            pltpu.VMEM(local_params.shape[1:], BF16),
            pltpu.VMEM((rows, columns), BF16),
            pltpu.VMEM(momentum.shape, F32),
            pltpu.VMEM((length, width), BF16),
            pltpu.VMEM(keyvals.shape[1:], BF16),
            pltpu.VMEM((1, length), jnp.int32),
            pltpu.VMEM((length, 2 * HEAD), BF16),
            pltpu.VMEM((BLOCK, BLOCK + SPAN), F32),
            pltpu.VMEM((GROUP, ROWS, columns), BF16),
            pltpu.VMEM((TWINS, ROWS, columns), BF16),
            pltpu.VMEM((GROUP, ROWS, columns), BF16),
            pltpu.VMEM((SHEET, COLUMN, ROWS, columns // 4), BF16),
            pltpu.VMEM((rows, columns), F32),
            pltpu.VMEM((ROWS, columns), F32),
            pltpu.VMEM((LINE, 1, 128), F32),
            pltpu.VMEM((PLANE, 1, 128), F32),
            dma((11,)),
            dma((GROUP,)), dma((GROUP,)),
            dma((TWINS,)), dma((TWINS,)),
            dma((GROUP,)), dma((GROUP,)),
            dma((COLUMN,)), dma((COLUMN,)),
            dma((SHEET,)), dma((SHEET,)),
            dma((LINE,)), dma((LINE,)),
            dma((PLANE,)), dma((PLANE,)),
        ],
        compiler_params=pltpu.CompilerParams(
            collective_id=0, has_side_effects=True, vmem_limit_bytes=56 * 1024 * 1024
        ),
    )(global_start, local_params, layer_index, momentum, queries, keyvals, segment_ids)
    return pl.pallas_call(
        settle,
        out_shape=out_shape,
        in_specs=[far] * 3,
        out_specs=(far,) * 3,
        scratch_shapes=[
            pltpu.VMEM(momentum.shape, F32),
            pltpu.VMEM((rows, columns), BF16),
            pltpu.VMEM((length, width), BF16),
            dma((2, 6)),
        ],
        compiler_params=pltpu.CompilerParams(vmem_limit_bytes=60 * 1024 * 1024),
    )(*results)


def solution(mesh):
    in_specs = (
        P(None, "tensor"),
        P("replica", None, None, "tensor"),
        P("replica"),
        P("replica", "tensor"),
        P("replica", None, "tensor"),
        P("replica", None, None, "tensor"),
        P("replica", None),
    )
    out_specs = (P("replica", "tensor"), P("replica", None, "tensor"), P("replica", None, "tensor"))
    return jax.shard_map(shards, mesh=mesh, in_specs=in_specs, out_specs=out_specs, check_vma=False)
```

```python
import jax
import jax.numpy as jnp
from jax import lax
from jax.experimental import pallas as pl
from jax.experimental.pallas import tpu as pltpu
from jax.sharding import PartitionSpec as P

D = 8192
FRAG = 256
REPLICAS = 64
MESH = pl.DeviceIdType.MESH
ROWS = 16
GROUP = 16
TWINS = 4
PLANE = 16
LINE = 8
COLUMN = 8
SHEET = 8
BLOCK = 256
HEAD = 128
SPAN = 512
FAR16 = (11, 10, 9, 15, 7, 8, 14, 13, 6, 5, 3, 12, 4, 2, 1)
FAR8 = (4, 3, 5, 2, 6, 1, 7)
FAR4 = (2, 1, 3)
SHEETS = (5, 4, 7, 3, 6, 2, 1)
F32 = jnp.float32
BF16 = jnp.bfloat16


def fused(
    start_hbm, params_hbm, slot_hbm, moment_hbm, query_hbm, keyval_hbm, segment_hbm,
    newmom_hbm, blended_hbm, attended_hbm,
    newmom, blended, attended, slot_ref, start, params, layer, moment, query, keyval, segment, values, bias,
    reduce_buf, twin_buf, average, mom_all, base_full, piece, sum_one, sum_two,
    local_sem, reduce_s, reduce_r, twin_s, twin_r, gather_s, gather_r,
    momone_s, momone_r, momtwo_s, momtwo_r, sumone_s, sumone_r, sumtwo_s, sumtwo_r,
):
    replica = lax.axis_index("replica")
    tensor = lax.axis_index("tensor")
    xs, twin, low = lax.div(replica, 16), lax.rem(lax.div(replica, 4), TWINS), lax.rem(replica, 4)
    zl, yl = lax.div(low, 2), lax.rem(low, 2)
    yh, core = lax.div(tensor, 2), lax.rem(tensor, 2)
    mine = xs * 4 + low
    plane = xs * 4 + zl * 2 + core
    line = yh * 2 + yl
    column = twin * 2 + zl
    sheet = xs * 2 + yl

    x_at = [xs] + [lax.rem(xs + d, 4) for d in (1, 2, 3)]
    z_at, y_at, core_at = (zl * 2, 2 - zl * 2), (yl, 1 - yl), (core, 1 - core)
    twin_at = [twin] + [lax.rem(twin + d, TWINS) for d in (1, 2, 3)]
    column_at = [column] + [lax.rem(column + d, COLUMN) for d in range(1, COLUMN)]
    line_at = [line] + [lax.rem(line + d, LINE) for d in range(1, LINE)]
    x_four, x_two = [x * 4 for x in x_at], [x * 2 for x in x_at]
    x_member = [x * 16 + twin * 4 for x in x_at]
    x_sheet = [x * 16 + column * 2 for x in x_at]
    rest = replica - yl

    def off16(k):
        return x_four[k // 4] + (z_at[k // 2 % 2] + y_at[k % 2])

    def off_plane(k):
        return x_four[k // 4] + (z_at[k // 2 % 2] + core_at[k % 2])

    def off_sheet(k):
        return x_two[k // 2] + y_at[k % 2]

    def back(k, pair):
        return (4 - k // pair) % 4 * pair + k % pair

    def member(k):
        return (x_member[k // 4] + (z_at[k // 2 % 2] + y_at[k % 2]), tensor)

    def twin_of(k):
        return (xs * 16 + low + twin_at[k] * 4, tensor)

    def plane_of(k):
        return (x_member[k // 4] + (z_at[k // 2 % 2] + yl), yh * 2 + core_at[k % 2])

    def line_of(k):
        return (rest + lax.rem(line_at[k], 2), line_at[k] - lax.rem(line_at[k], 2) + core)

    def column_of(k):
        return (xs * 16 + yl + column_at[k] * 2, tensor)

    def sheet_of(k):
        return (x_sheet[k // 2] + y_at[k % 2], tensor)

    def rows_of(g):
        return pl.ds(pl.multiple_of(g * ROWS, ROWS), ROWS)

    def remote(src, dst, send, recv, device):
        return pltpu.make_async_remote_copy(
            src_ref=src, dst_ref=dst, send_sem=send, recv_sem=recv,
            device_id=device, device_id_type=MESH,
        )

    def reduce_copy(k):
        return remote(layer.at[rows_of(off16(k))], reduce_buf.at[mine], reduce_s.at[k], reduce_r.at[mine], member(k))

    def twin_copy(k):
        return remote(twin_buf.at[twin], twin_buf.at[twin], twin_s.at[k], twin_r.at[twin], twin_of(k))

    def gather_copy(k):
        return remote(average.at[mine], average.at[mine], gather_s.at[k], gather_r.at[mine], member(k))

    def momone_copy(k):
        own = mom_all.at[sheet, column]
        return remote(own, own, momone_s.at[k], momone_r.at[column], column_of(k))

    def momtwo_copy(k):
        return remote(mom_all.at[sheet], mom_all.at[sheet], momtwo_s.at[k], momtwo_r.at[sheet], sheet_of(k))

    def sumone_copy(k):
        return remote(sum_one.at[line], sum_one.at[line], sumone_s.at[k], sumone_r.at[line], line_of(k))

    def sumtwo_copy(k):
        return remote(sum_two.at[plane], sum_two.at[plane], sumtwo_s.at[k], sumtwo_r.at[plane], plane_of(k))

    def each(order, act):
        for k in order:
            act(k)

    def arrived(slots, sems, slot):
        pltpu.make_async_copy(slots.at[slot], slots.at[slot], sems.at[slot]).wait()

    loads = [
        pltpu.make_async_copy(params_hbm.at[0], params, local_sem.at[0]),
        pltpu.make_async_copy(moment_hbm, moment, local_sem.at[1]),
        pltpu.make_async_copy(start_hbm, start, local_sem.at[2]),
        pltpu.make_async_copy(segment_hbm, segment, local_sem.at[3]),
        pltpu.make_async_copy(keyval_hbm.at[0], keyval, local_sem.at[4]),
        pltpu.make_async_copy(query_hbm.at[0], query, local_sem.at[5]),
    ]
    barrier = pltpu.get_barrier_semaphore()

    def greet(device):
        pl.semaphore_signal(barrier, inc=1, device_id=device, device_id_type=MESH)

    each(FAR16, lambda k: greet(member(k)))
    loads[0].start()
    index = pltpu.make_async_copy(slot_hbm, slot_ref, local_sem.at[10])
    index.start()
    for k in FAR8:
        if k % 2 == 0:
            greet(column_of(k))
            greet(line_of(k))
    for d in (1, 2, 3):
        greet((xs * 16 + yl + twin_at[d] * 4 + z_at[1], tensor))
        greet((rest + y_at[1], lax.rem(yh + d, 4) * 2 + core))
    each(range(1, 16, 2), lambda k: greet(plane_of(k)))
    for load in loads[1:]:
        load.start()

    loads[0].wait()
    index.wait()
    slot = slot_ref[0]
    layer[...] = params[slot]
    loads[1].wait()
    fold = moment.shape[1] // 4
    for j in range(4):
        piece[4 * j:4 * j + 4, :fold] = moment[:, j * fold:(j + 1) * fold]
    mom_all[sheet, column] = piece[:, :fold].astype(BF16)
    pl.semaphore_wait(barrier, GROUP + COLUMN + PLANE // 2 + LINE - 5)

    each(FAR8, lambda k: momone_copy(k).start())

    each(FAR16, lambda k: reduce_copy(k).start())
    for load in loads[3:]:
        load.wait()
    values[:, :HEAD] = keyval[1]
    values[:, HEAD:] = jnp.ones((values.shape[0], HEAD), BF16)
    scale = 1.4426950408889634 / (HEAD ** 0.5)

    def attend(block):
        first, last = block * BLOCK, (block + 1) * BLOCK
        begin = max(0, first - SPAN)
        width = last - begin
        own = jnp.broadcast_to(segment[:, first:last], (BLOCK, BLOCK)).T
        for at in range(begin, last, BLOCK):
            keep = own == segment[:, at:at + BLOCK]
            if at == first:
                row = lax.broadcasted_iota(jnp.int32, (BLOCK, BLOCK), 0)
                col = lax.broadcasted_iota(jnp.int32, (BLOCK, BLOCK), 1)
                keep = keep & (col <= row)
            bias[:, at - begin:at - begin + BLOCK] = jnp.where(keep, 0.0, -1e30).astype(F32)

        def head(h, carry):
            columns = pl.ds(pl.multiple_of(h * HEAD, HEAD), HEAD)
            scores = lax.dot_general(
                query[first:last, columns], keyval[0, begin:last, :],
                (((1,), (1,)), ((), ())), preferred_element_type=F32,
            )
            scores = scores * scale + bias[:, :width]
            peak = jnp.max(scores, axis=1, keepdims=True)
            expo = jnp.exp2(scores - peak).astype(BF16)
            out = jnp.dot(expo, values[begin:last, :], preferred_element_type=F32)
            attended[first:last, columns] = (out[:, :HEAD] / out[:, HEAD:]).astype(BF16)
            return carry

        lax.fori_loop(0, query.shape[1] // HEAD, head, 0)

    attend(3)
    attend(2)

    loads[2].wait()
    base = start[rows_of(mine), :].astype(F32)

    partial = base - layer[rows_of(mine), :].astype(F32)
    for k in FAR16:
        place = off16(back(k, 4))
        arrived(reduce_buf, reduce_r, place)
        partial = partial + (base - reduce_buf[place].astype(F32))
    twin_buf[twin] = partial.astype(BF16)
    each(FAR4, lambda k: twin_copy(k).start())

    each(FAR8, lambda k: arrived(mom_all.at[sheet], momone_r, column_at[COLUMN - k]))
    each(SHEETS, lambda k: momtwo_copy(k).start())

    attend(1)
    attend(0)
    attended_out = pltpu.make_async_copy(attended, attended_hbm.at[0], local_sem.at[6])
    attended_out.start()

    each(FAR4, lambda k: arrived(twin_buf, twin_r, twin_at[TWINS - k]))
    total = twin_buf[0].astype(F32)
    for t in range(1, TWINS):
        total = total + twin_buf[t].astype(F32)
    total = total * (1.0 / REPLICAS)
    average[mine] = total.astype(BF16)
    square = total * total
    parts = square[0:8, 0:128]
    for r in range(0, ROWS, 8):
        for c in range(0, square.shape[1], 128):
            if r or c:
                parts = parts + square[r:r + 8, c:c + 128]
    sum_one[line] = jnp.sum(parts, axis=0, keepdims=True)
    each(FAR8, lambda k: sumone_copy(k).start())
    each(FAR16, lambda k: gather_copy(k).start())

    each(FAR8, lambda k: arrived(sum_one, sumone_r, line_at[LINE - k]))
    parts = sum_one[0]
    for y in range(1, LINE):
        parts = parts + sum_one[y]
    sum_two[plane] = parts
    each(FAR16, lambda k: sumtwo_copy(k).start())

    each(SHEETS, lambda k: arrived(mom_all, momtwo_r, off_sheet(back(k, 2))))
    for p in range(SHEET):
        for z in range(COLUMN):
            piece[:, :fold] = mom_all[p, z].astype(F32)
            at = ((p // 2) * 16 + z * 2 + p % 2) * 4
            for j in range(4):
                base_full[at:at + 4, j * fold:(j + 1) * fold] = piece[4 * j:4 * j + 4, :fold]

    def ahead(c, carry):
        rows = rows_of(c)
        base_full[rows, :] = start[rows, :].astype(F32) - (0.7 * 0.9 * 0.9) * base_full[rows, :]
        return carry

    lax.fori_loop(0, GROUP, ahead, 0)

    each(FAR16, lambda k: reduce_copy(k).wait_send())
    each(FAR4, lambda k: twin_copy(k).wait_send())
    each(FAR16, lambda k: gather_copy(k).wait_send())
    each(FAR8, lambda k: momone_copy(k).wait_send())
    each(SHEETS, lambda k: momtwo_copy(k).wait_send())
    each(FAR8, lambda k: sumone_copy(k).wait_send())
    each(FAR16, lambda k: arrived(average, gather_r, off16(back(k, 4))))
    each(FAR16, lambda k: arrived(sum_two, sumtwo_r, off_plane(back(k, 4))))
    parts = sum_two[0]
    for p in range(1, PLANE):
        parts = parts + sum_two[p]
    square = jnp.sum(parts, axis=1, keepdims=True)
    factor = lax.rsqrt(square * (1.0 / (FRAG * D)) + 1e-06)
    step = factor * (0.7 * 1.9)

    def update(c, carry):
        rows = rows_of(c)
        fresh = (base_full[rows, :] - average[c].astype(F32) * step).astype(BF16)
        blended[rows, :] = (0.5 * (layer[rows, :].astype(F32) + fresh.astype(F32))).astype(BF16)
        return carry

    outs = []
    for part in range(2):
        lax.fori_loop(part * GROUP // 2, (part + 1) * GROUP // 2, update, 0, unroll=True)
        span = pl.ds(part * ROWS * GROUP // 2, ROWS * GROUP // 2)
        outs.append(pltpu.make_async_copy(blended.at[span], blended_hbm.at[0, span], local_sem.at[7 + part]))
        outs[-1].start()

    piece[...] = average[lax.div(replica, 4)].astype(F32)
    own = piece[0:4, :]
    for t in range(1, 4):
        own = jnp.where(low == t, piece[4 * t:4 * t + 4, :], own)
    newmom[...] = 0.9 * moment[...] + own * factor
    outs.append(pltpu.make_async_copy(newmom, newmom_hbm, local_sem.at[9]))
    outs[-1].start()

    each(FAR16, lambda k: sumtwo_copy(k).wait_send())
    attended_out.wait()
    for out in outs:
        out.wait()


def settle(newmom_in, blended_in, attended_in, newmom_out, blended_out, attended_out, newmom, blended, attended, sem):
    pieces = [(newmom_in, newmom, newmom_out)]
    for source, stage, target in ((attended_in, attended, attended_out), (blended_in, blended, blended_out)):
        for at in range(0, source.shape[1], 256):
            span = pl.ds(at, 256)
            pieces.append((source.at[0, span], stage.at[span], target.at[0, span]))
    into = [pltpu.make_async_copy(p[0], p[1], sem.at[0, i]) for i, p in enumerate(pieces)]
    out = [pltpu.make_async_copy(p[1], p[2], sem.at[1, i]) for i, p in enumerate(pieces)]
    for copy in into:
        copy.start()
    for i in range(len(pieces)):
        into[i].wait()
        out[i].start()
    for copy in out:
        copy.wait()


def shards(global_start, local_params, layer_index, momentum, queries, keyvals, segment_ids):
    rows, columns = global_start.shape
    length, width = queries.shape[1:]
    far = pl.BlockSpec(memory_space=pl.ANY)
    dma = pltpu.SemaphoreType.DMA
    out_shape = (
        jax.ShapeDtypeStruct(momentum.shape, F32),
        jax.ShapeDtypeStruct((1, rows, columns), BF16),
        jax.ShapeDtypeStruct(queries.shape, BF16),
    )
    results = pl.pallas_call(
        fused,
        out_shape=out_shape,
        in_specs=[far, far, far, far, far, far, far],
        out_specs=(far, far, far),
        scratch_shapes=[
            pltpu.VMEM(momentum.shape, F32),
            pltpu.VMEM((rows, columns), BF16),
            pltpu.VMEM((length, width), BF16),
            pltpu.SMEM((1,), jnp.int32),
            pltpu.VMEM((rows, columns), BF16),
            pltpu.VMEM(local_params.shape[1:], BF16),
            pltpu.VMEM((rows, columns), BF16),
            pltpu.VMEM(momentum.shape, F32),
            pltpu.VMEM((length, width), BF16),
            pltpu.VMEM(keyvals.shape[1:], BF16),
            pltpu.VMEM((1, length), jnp.int32),
            pltpu.VMEM((length, 2 * HEAD), BF16),
            pltpu.VMEM((BLOCK, BLOCK + SPAN), F32),
            pltpu.VMEM((GROUP, ROWS, columns), BF16),
            pltpu.VMEM((TWINS, ROWS, columns), BF16),
            pltpu.VMEM((GROUP, ROWS, columns), BF16),
            pltpu.VMEM((SHEET, COLUMN, ROWS, columns // 4), BF16),
            pltpu.VMEM((rows, columns), F32),
            pltpu.VMEM((ROWS, columns), F32),
            pltpu.VMEM((LINE, 1, 128), F32),
            pltpu.VMEM((PLANE, 1, 128), F32),
            dma((11,)),
            dma((GROUP,)), dma((GROUP,)),
            dma((TWINS,)), dma((TWINS,)),
            dma((GROUP,)), dma((GROUP,)),
            dma((COLUMN,)), dma((COLUMN,)),
            dma((SHEET,)), dma((SHEET,)),
            dma((LINE,)), dma((LINE,)),
            dma((PLANE,)), dma((PLANE,)),
        ],
        compiler_params=pltpu.CompilerParams(
            collective_id=0, has_side_effects=True, vmem_limit_bytes=56 * 1024 * 1024
        ),
    )(global_start, local_params, layer_index, momentum, queries, keyvals, segment_ids)
    return pl.pallas_call(
        settle,
        out_shape=out_shape,
        in_specs=[far] * 3,
        out_specs=(far,) * 3,
        scratch_shapes=[
            pltpu.VMEM(momentum.shape, F32),
            pltpu.VMEM((rows, columns), BF16),
            pltpu.VMEM((length, width), BF16),
            dma((2, 6)),
        ],
        compiler_params=pltpu.CompilerParams(vmem_limit_bytes=60 * 1024 * 1024),
    )(*results)


def solution(mesh):
    in_specs = (
        P(None, "tensor"),
        P("replica", None, None, "tensor"),
        P("replica"),
        P("replica", "tensor"),
        P("replica", None, "tensor"),
        P("replica", None, None, "tensor"),
        P("replica", None),
    )
    out_specs = (P("replica", "tensor"), P("replica", None, "tensor"), P("replica", None, "tensor"))
    return jax.shard_map(shards, mesh=mesh, in_specs=in_specs, out_specs=out_specs, check_vma=False)
```
